256 devices in a mesh: seq: 64 (over z, y, core), head: 4 (over x).
Axes of the slice: x: 4, y: 4, z: 8, core: 2. Of those that a mesh axis runs over, the one named last changes fastest.
Arguments:
- queries: bfloat16 [24576, 4096], P(('seq', 'head')), may hold values from -5 to 5
- keys: bfloat16 [24576, 1024], P(('seq', 'head')), may hold values from -5 to 5
- values: bfloat16 [24576, 1024], P(('seq', 'head')), may hold values from -6 to 6
- out_grad: bfloat16 [24576, 4096], P(('seq', 'head')), may hold values from -6 to 6
- lengths: int32 [32], replicated, may hold values from 1 to 16, 256 in all
Outputs:
- query_grad: bfloat16 [24576, 4096], P(('seq', 'head'))
- key_grad: bfloat16 [24576, 1024], P(('seq', 'head'))
- value_grad: bfloat16 [24576, 1024], P(('seq', 'head'))
The draws below stay inside these ranges and needn't reach their ends.
Inputs may be any that keep to these rules, and one draw needn't show every extreme that they name: Documents fill the sequence: the lengths sum to 256, and one or more documents have the largest length 16.
All inputs are finite; a program needn't handle non-finite values.
Results may differ from the reference program's by a relative error of at most 0.04.
Values may be sent and summed in bfloat16 or wider, within the bound.
A program may use at most 128 MiB of HBM per device.

```python
import math
import jax
import jax.numpy as jnp
import numpy as np
from jax import lax

QH = 32
KVH = 8
HD = 128
TOK_DEV = 384
REACH = 4
UNIT = 96
TOKENS = 24576
NDOCS = 32


def draw_keys(key, part):
    key = jax.random.fold_in(key, 21)
    base = jnp.clip(jax.random.normal(key, (TOKENS, KVH, HD), jnp.float32), -5.0, 5.0)
    return base.reshape(TOKENS, KVH * HD).astype(jnp.bfloat16)


def draw_queries(key, part):
    key = jax.random.fold_in(key, 33)
    base = jnp.clip(jax.random.normal(key, (TOKENS, KVH, QH // KVH, HD), jnp.float32), -5.0, 5.0)
    return base.reshape(TOKENS, QH * HD).astype(jnp.bfloat16)


def shard_levels(own_key, extent, split, least, high):
    def one(axis_at, parts):
        draws = jax.random.uniform(jax.random.fold_in(jax.random.fold_in(own_key, 6), axis_at), (parts,), jnp.float32, least / len(split), high / len(split))
        return jnp.repeat(jnp.exp(draws), extent[axis_at] // parts).reshape((-1,) + (1,) * (len(extent) - axis_at - 1))

    gain = one(*split[0])
    for cut in split[1:]:
        gain = gain * one(*cut)
    return gain


def split_up(count, total, reach, slope):
    weights = [(1 << 20) // math.isqrt(standing ** slope) + 1 for standing in range(2, count + 1)]
    rest, given = total - reach - (count - 1), [1] * (count - 1)
    while rest > 0:
        candidates = [i for i in range(count - 1) if given[i] < reach]
        mass, budget = sum([weights[i] for i in candidates]), rest
        for i in candidates:
            addition = min(reach - given[i], max(1, budget * weights[i] // mass), rest)
            given[i] = given[i] + addition
            rest = rest - addition
    return np.array([reach] + given)


def uneven(rng, amount, total, limit, skew):
    if amount == 2:
        one = jax.random.randint(rng, (), max(1, total - limit), min(limit, total - 1) + 1)
        return jnp.stack([one, total - one])
    sizes = jnp.asarray(split_up(amount, total, limit, skew), jnp.int32)
    couples = (amount - 1) // 2
    donor, sink = sizes[1:1 + 2 * couples:2], sizes[2:2 + 2 * couples:2]
    slack = jnp.minimum(donor - 1, limit - sink)
    moved = jax.random.randint(jax.random.fold_in(rng, 1), (couples,), 0, 1 << 20) % (slack + 1)
    sizes = sizes.at[1:1 + 2 * couples:2].set(donor - moved).at[2:2 + 2 * couples:2].set(sink + moved)
    return sizes[jax.random.permutation(jax.random.fold_in(rng, 2), amount)]


def noise(stream_key, shape, deviation, limit, cuts=(), kind=jnp.bfloat16):
    values = jax.random.normal(stream_key, shape, jnp.float32) * deviation
    if len(cuts) > 0:
        values = shard_levels(stream_key, shape, cuts, -0.22, 0.18) * values
    return jnp.clip(values, min=-limit, max=limit).astype(kind)


def setup_inputs(seed: int = 0) -> dict:
    key_list = jax.random.split(jax.random.key(seed), 6)
    return {
        "queries": draw_queries(jax.random.fold_in(key_list[5], 71), 0),
        "keys": draw_keys(jax.random.fold_in(key_list[5], 71), 0),
        "values": noise(key_list[2], (TOKENS, KVH * HD), 1.0, 6.0, ((0, 256),)),
        "out_grad": noise(key_list[3], (TOKENS, QH * HD), 1.0, 6.0, ((0, 256),)),
        "lengths": uneven(key_list[4], NDOCS, TOKENS // UNIT, 4 * REACH, 2).astype(jnp.int32),
    }


def doc_index(positions, bounds):
    return lax.optimization_barrier(jnp.sum((positions[:, None] >= bounds[None, :]).astype(jnp.int32), axis=1)).astype(jnp.int32)

def round_low(array):
    return lax.optimization_barrier(array.astype(jnp.bfloat16)).astype(jnp.float32)

def reference(queries, keys, values, out_grad, lengths):
    groups = QH // KVH
    scale = 1.0 / math.sqrt(HD)
    block = TOK_DEV
    margin = REACH * block
    highest = lax.Precision.HIGHEST
    bounds = (jnp.cumsum(lengths) * UNIT).astype(jnp.int32)
    query_all = queries.reshape(TOKENS, KVH, groups, HD)
    grad_all = out_grad.reshape(TOKENS, KVH, groups, HD)
    front = jnp.zeros((margin, KVH, HD), keys.dtype)
    key_all = jnp.concatenate([front, keys.reshape(TOKENS, KVH, HD)], axis=0)
    value_all = jnp.concatenate([front, values.reshape(TOKENS, KVH, HD)], axis=0)

    def step(carry, index):
        key_acc, value_acc = carry
        start = (index * block).astype(jnp.int32)
        qrows = lax.dynamic_slice_in_dim(query_all, start, block, 0).astype(jnp.float32)
        grows = lax.dynamic_slice_in_dim(grad_all, start, block, 0).astype(jnp.float32)
        krows = lax.dynamic_slice_in_dim(key_all, start, margin + block, 0).astype(jnp.float32)
        vrows = lax.dynamic_slice_in_dim(value_all, start, margin + block, 0).astype(jnp.float32)
        qpos = start + jnp.arange(block, dtype=jnp.int32)
        kpos = start - margin + jnp.arange(margin + block, dtype=jnp.int32)
        allowed = doc_index(qpos, bounds)[:, None] == doc_index(kpos, bounds)[None, :]
        allowed = allowed & (kpos[None, :] <= qpos[:, None]) & (kpos[None, :] >= 0)
        scores = jnp.einsum('tgjd,ugd->gjtu', qrows, krows, precision=highest) * scale
        masked = jnp.where(allowed, scores, -jnp.inf)
        top = lax.optimization_barrier(jnp.max(masked, axis=-1, keepdims=True))
        logsum = top + jnp.log(lax.optimization_barrier(jnp.sum(jnp.exp(masked - top), axis=-1, keepdims=True)))
        probs = jnp.where(allowed, jnp.exp(scores - logsum), 0.0)
        probs_fwd = round_low(probs)
        attended = jnp.einsum('gjtu,ugd->tgjd', probs_fwd, vrows, precision=highest)
        delta = jnp.transpose(lax.optimization_barrier(jnp.sum(grows * attended, axis=-1)), (1, 2, 0))[..., None]
        dprobs = jnp.einsum('tgjd,ugd->gjtu', grows, vrows, precision=highest)
        dscores = probs * (dprobs - delta)
        probs_low = round_low(probs)
        dscores_low = round_low(dscores)
        value_block = jnp.einsum('gjtu,tgjd->ugd', probs_low, grows, precision=highest)
        key_block = jnp.einsum('gjtu,tgjd->ugd', dscores_low, qrows, precision=highest) * scale
        query_block = jnp.einsum('gjtu,ugd->tgjd', dscores_low, krows, precision=highest) * scale
        old_keys = lax.dynamic_slice_in_dim(key_acc, start, margin + block, 0)
        old_values = lax.dynamic_slice_in_dim(value_acc, start, margin + block, 0)
        key_acc = lax.dynamic_update_slice_in_dim(key_acc, old_keys + key_block, start, 0)
        value_acc = lax.dynamic_update_slice_in_dim(value_acc, old_values + value_block, start, 0)
        return ((key_acc, value_acc), query_block.astype(jnp.bfloat16))
    empty = jnp.zeros((TOKENS + margin, KVH, HD), jnp.float32)
    (key_acc, value_acc), query_blocks = lax.scan(step, (empty, empty), jnp.arange(TOKENS // block, dtype=jnp.int32))
    query_grad = query_blocks.reshape(TOKENS, QH * HD)
    key_grad = key_acc[margin:].astype(jnp.bfloat16).reshape(TOKENS, KVH * HD)
    value_grad = value_acc[margin:].astype(jnp.bfloat16).reshape(TOKENS, KVH * HD)
    return (query_grad, key_grad, value_grad)
```

```python
import functools
import math

import jax
import jax.numpy as jnp
from jax import lax
from jax.experimental import pallas as pl
from jax.experimental.pallas import tpu as pltpu
from jax.sharding import PartitionSpec as P

MESH = pl.DeviceIdType.MESH
HD = 128
U = 96
NX = 4
SH = NX * U
REACH = 4
WIN = (REACH + 1) * SH
KVL = 2
GR = 4
QT = 256
TILES = GR * SH // QT
ROWS = 17 * U
NEG = -1e30
SCALE = 1.0 / math.sqrt(HD)
EXP2_SCALE = SCALE * math.log2(math.e)
NT = (((1,), (1,)), ((), ()))
TN = (((0,), (0,)), ((), ()))
F32 = jnp.float32
BF16 = jnp.bfloat16


def kernel(
    n_seq,
    lengths, q_in, k_in, v_in, o_in,
    dq_out, dk_out, dv_out,
    kvw, qb, ob, qst, ost, s_buf, d_buf, p_low, s_low, acc, stage, landed, dq_stage, final,
    local_sem, kv_send, kv_recv, qo_send, qo_recv, ctx_send, ctx_recv, ret_send, ret_recv,
    out_send, out_recv,
):
    s = lax.axis_index("seq")
    x = lax.axis_index("head")
    core = lax.rem(s, 2)
    sibling = s + 1 - 2 * core
    ahead = lax.rem(s + 2, n_seq)
    behind = lax.rem(s + n_seq - 2, n_seq)
    peers = [lax.rem(x + d, NX) for d in range(NX)]

    barrier = pltpu.get_barrier_semaphore()
    for d in range(1, NX):
        pl.semaphore_signal(barrier, inc=1, device_id=(s, peers[d]), device_id_type=MESH)
    for other in (sibling, ahead, behind):
        pl.semaphore_signal(barrier, inc=1, device_id=(other, x), device_id_type=MESH)
    pl.semaphore_wait(barrier, NX + 2)

    def remote(src, dst, send, recv, where):
        return pltpu.make_async_remote_copy(
            src_ref=src, dst_ref=dst, send_sem=send, recv_sem=recv,
            device_id=where, device_id_type=MESH,
        )

    def rows(start, size):
        return pl.ds(pl.multiple_of(start, U), size)

    def lanes(start, size):
        return pl.ds(pl.multiple_of(start, HD), size)

    def kv_copy(h, t, d):
        src = (k_in, v_in)[t].at[:, lanes(peers[d] * KVL * HD + h * HD, HD)]
        dst = kvw.at[h, t, rows(REACH * SH + x * U, U), :]
        if d == 0:
            return pltpu.make_async_copy(src, dst, local_sem.at[h, t])
        i = d - 1
        return remote(src, dst, kv_send.at[h, t, i], kv_recv.at[h, t, i], (s, peers[d]))

    def qo_copy(h, t, d):
        wide = GR * HD
        src = (q_in, o_in)[t].at[:, lanes(peers[d] * KVL * wide + h * wide, wide)]
        dst = (qb, ob)[t].at[h, x]
        if d == 0:
            return pltpu.make_async_copy(src, dst, local_sem.at[h, 2 + t])
        i = d - 1
        return remote(src, dst, qo_send.at[h, t, i], qo_recv.at[h, t, i], (s, peers[d]))

    def shard(rel):
        return rows((REACH + rel) * SH, SH)

    def own_ahead(h):
        return remote(kvw.at[h, :, shard(0), :], kvw.at[h, :, shard(-2), :],
                      ctx_send.at[h, 0], ctx_recv.at[h, 0], (ahead, x))

    def relay_ahead(h):
        return remote(kvw.at[h, :, shard(-2), :], kvw.at[h, :, shard(-4), :],
                      ctx_send.at[h, 1], ctx_recv.at[h, 1], (ahead, x))

    def share_near(h):
        return remote(kvw.at[h, :, shard(-2 * core), :], kvw.at[h, :, shard(-1), :],
                      ctx_send.at[h, 2], ctx_recv.at[h, 2], (sibling, x))

    def share_far(h):
        return remote(kvw.at[h, :, shard(-2 - 2 * core), :], kvw.at[h, :, shard(-3), :],
                      ctx_send.at[h, 3], ctx_recv.at[h, 3], (sibling, x))

    for h in range(KVL):
        for d in (2, 1, 3, 0):
            for t in range(2):
                kv_copy(h, t, d).start()
    for h in range(KVL):
        for d in (2, 1, 3, 0):
            for t in range(2):
                qo_copy(h, t, d).start()

    def wait_in(h, copy):
        for t in range(2):
            copy(h, t, 0).wait()
            for d in range(1, NX):
                copy(h, t, d).wait_recv()

    for h in range(KVL):
        wait_in(h, kv_copy)
        own_ahead(h).start()

        @pl.when(core == 0)
        def _():
            share_near(h).start()

    first_unit = s * NX - REACH * NX
    starts = [jnp.int32(-(1 << 20))] * NX
    bound = jnp.int32(0)
    starts = [jnp.int32(0) - first_unit] * NX
    for doc in range(lengths.shape[0]):
        bound = bound + lengths[doc]
        starts = [
            jnp.where(bound <= s * NX + a, bound - first_unit, starts[a]) for a in range(NX)
        ]

    for h in range(KVL):
        own_ahead(h).wait_recv()
        relay_ahead(h).start()

        @pl.when(core == 0)
        def _():
            share_far(h).start()

        @pl.when(core == 1)
        def _():
            share_near(h).start()

    for h in range(KVL):
        relay_ahead(h).wait_recv()

        @pl.when(core == 1)
        def _():
            share_far(h).start()

    acc[...] = jnp.zeros_like(acc)
    for h in range(KVL):
        wait_in(h, qo_copy)
        for a in range(NX):
            for j in range(GR):
                at = (a * GR + j) * U
                qst[h, at:at + U, :] = qb[h, a, :, j * HD:(j + 1) * HD]
                ost[h, at:at + U, :] = ob[h, a, :, j * HD:(j + 1) * HD]
    for h in range(KVL):
        share_near(h).wait_recv()
        share_far(h).wait_recv()

    lane = lax.broadcasted_iota(jnp.int32, (1, QT), 1)
    row = lax.broadcasted_iota(jnp.int32, (U, QT), 0)

    def tile(i, carry):
        h = i // TILES
        tile_at = lax.rem(i, TILES)
        pair = tile_at // (TILES // 2)
        base = pl.multiple_of((1 + 2 * pair) * U, U)
        cols = tile_at * QT + lane
        unit = cols // (GR * U)
        at = lax.rem(cols, U)
        begin = jnp.zeros((1, QT), jnp.int32)
        for a in range(NX):
            begin = jnp.where(unit == a, starts[a], begin)
        tile_rows = pl.ds(pl.multiple_of(tile_at * QT, QT), QT)
        q_tile = qst[h, tile_rows, :]
        o_tile = ost[h, tile_rows, :]

        def bias(b):
            return jnp.where((begin <= b) & (b <= REACH * NX + unit), 0.0, NEG)

        top = jnp.full((8, QT), -3e38, F32)
        for c in range(ROWS // U):
            b = 1 + 2 * pair + c
            keys = kvw[h, 0, pl.ds(base + c * U, U), :]
            scores = lax.dot_general(keys, q_tile, NT, preferred_element_type=F32)
            if c >= 15:
                ok = (b < REACH * NX + unit) | (row <= at)
                scores = jnp.where(ok, scores, NEG)
            s_buf[c * U:(c + 1) * U, :] = scores
            top = jnp.maximum(top, jnp.max(scores.reshape(U // 8, 8, QT), axis=0) + bias(b))
        top = jnp.max(top, axis=0, keepdims=True)

        total = jnp.zeros((8, QT), F32)
        inner = jnp.zeros((8, QT), F32)
        for c in range(ROWS // U):
            b = 1 + 2 * pair + c
            shift = (bias(b) - top) * EXP2_SCALE
            weights = jnp.exp2(s_buf[c * U:(c + 1) * U, :] * EXP2_SCALE + shift)
            vals = kvw[h, 1, pl.ds(base + c * U, U), :]
            dprobs = lax.dot_general(vals, o_tile, NT, preferred_element_type=F32)
            s_buf[c * U:(c + 1) * U, :] = weights
            d_buf[c * U:(c + 1) * U, :] = dprobs
            total = total + jnp.sum(weights.reshape(U // 8, 8, QT), axis=0)
            inner = inner + jnp.sum((weights * dprobs).reshape(U // 8, 8, QT), axis=0)
        inverse = 1.0 / jnp.sum(total, axis=0, keepdims=True)
        delta = jnp.sum(inner, axis=0, keepdims=True) * inverse

        for c in range(ROWS // U):
            probs = s_buf[c * U:(c + 1) * U, :] * inverse
            dscores = probs * (d_buf[c * U:(c + 1) * U, :] - delta)
            p_low[c * U:(c + 1) * U, :] = probs.astype(BF16)
            s_low[c * U:(c + 1) * U, :] = dscores.astype(BF16)
        window = pl.ds(base, ROWS)
        acc[h, 1, window, :] += jnp.dot(p_low[...], o_tile, preferred_element_type=F32)
        acc[h, 0, window, :] += jnp.dot(s_low[...], q_tile, preferred_element_type=F32)
        dq = lax.dot_general(
            s_low[...], kvw[h, 0, window, :], TN, preferred_element_type=F32
        )
        dq_stage[h, tile_rows, :] = (dq * SCALE).astype(BF16)
        return carry

    lax.fori_loop(0, KVL * TILES, tile, 0)

    wide = GR * HD

    def dq_copy(h, d):
        src = qb.at[h, peers[d]]
        dst = dq_out.at[:, lanes(x * KVL * wide + h * wide, wide)]
        if d == 0:
            return pltpu.make_async_copy(src, dst, local_sem.at[h, 4])
        return remote(src, dst, out_send.at[h, 0, d - 1], out_recv.at[h, 0, d - 1], (s, peers[d]))

    def dkv_copy(h, t, d):
        src = final.at[h, t, rows(peers[d] * U, U), :]
        dst = (dk_out, dv_out)[t].at[:, lanes(x * KVL * HD + h * HD, HD)]
        if d == 0:
            return pltpu.make_async_copy(src, dst, local_sem.at[h, 5 + t])
        i = d - 1
        return remote(
            src, dst, out_send.at[h, 1 + t, i], out_recv.at[h, 1 + t, i], (s, peers[d])
        )

    def ret_copy(h, n):
        where = ((sibling, x), (sibling, x), (behind, x), (behind, x))[n]
        return remote(stage.at[h, n], landed.at[h, n], ret_send.at[h, n], ret_recv.at[h, n], where)

    def put(h, n, rel):
        stage[h, n] = acc[h, :, shard(rel), :].astype(BF16)
        ret_copy(h, n).start()

    def take(h, n, rel):
        ret_copy(h, n).wait_recv()
        acc[h, :, shard(rel), :] += landed[h, n].astype(F32)

    for h in range(KVL):
        put(h, 0, -3)
        put(h, 1, -1)
        for a in range(NX):
            for j in range(GR):
                at = (a * GR + j) * U
                qb[h, a, :, j * HD:(j + 1) * HD] = dq_stage[h, at:at + U, :]
        for d in (2, 1, 3, 0):
            dq_copy(h, d).start()
    for h in range(KVL):
        take(h, 0, -2 - 2 * core)
        put(h, 2, -4)
        take(h, 1, -2 * core)
    for h in range(KVL):
        take(h, 2, -2)
        put(h, 3, -2)
    for h in range(KVL):
        take(h, 3, 0)
        final[h, 0] = (acc[h, 0, shard(0), :] * SCALE).astype(BF16)
        final[h, 1] = acc[h, 1, shard(0), :].astype(BF16)
        for d in (2, 1, 3, 0):
            for t in range(2):
                dkv_copy(h, t, d).start()

    for h in range(KVL):
        for d in range(1, NX):
            for t in range(2):
                kv_copy(h, t, d).wait_send()
                qo_copy(h, t, d).wait_send()
                dkv_copy(h, t, d).wait()
            dq_copy(h, d).wait()
        dq_copy(h, 0).wait()
        for t in range(2):
            dkv_copy(h, t, 0).wait()
        for copy in (own_ahead, relay_ahead, share_near, share_far):
            copy(h).wait_send()
        for n in range(4):
            ret_copy(h, n).wait_send()


def on_device(n_seq, queries, keys, values, out_grad, lengths):
    anywhere = pl.BlockSpec(memory_space=pl.ANY)
    dma = pltpu.SemaphoreType.DMA
    return pl.pallas_call(
        functools.partial(kernel, n_seq),
        out_shape=(
            jax.ShapeDtypeStruct(queries.shape, BF16),
            jax.ShapeDtypeStruct(keys.shape, BF16),
            jax.ShapeDtypeStruct(values.shape, BF16),
        ),
        in_specs=[pl.BlockSpec(memory_space=pltpu.SMEM)] + [anywhere] * 4,
        out_specs=(anywhere,) * 3,
        scratch_shapes=[
            pltpu.VMEM((KVL, 2, WIN, HD), BF16),
            pltpu.VMEM((KVL, NX, U, GR * HD), BF16),
            pltpu.VMEM((KVL, NX, U, GR * HD), BF16),
            pltpu.VMEM((KVL, GR * SH, HD), BF16),
            pltpu.VMEM((KVL, GR * SH, HD), BF16),
            pltpu.VMEM((ROWS, QT), F32),
            pltpu.VMEM((ROWS, QT), F32),
            pltpu.VMEM((ROWS, QT), BF16),
            pltpu.VMEM((ROWS, QT), BF16),
            pltpu.VMEM((KVL, 2, WIN, HD), F32),
            pltpu.VMEM((KVL, 4, 2, SH, HD), BF16),
            pltpu.VMEM((KVL, 4, 2, SH, HD), BF16),
            pltpu.VMEM((KVL, GR * SH, HD), BF16),
            pltpu.VMEM((KVL, 2, SH, HD), BF16),
            dma((KVL, 7)),
            dma((KVL, 2, NX - 1)), dma((KVL, 2, NX - 1)),
            dma((KVL, 2, NX - 1)), dma((KVL, 2, NX - 1)),
            dma((KVL, 4)), dma((KVL, 4)),
            dma((KVL, 4)), dma((KVL, 4)),
            dma((KVL, 3, NX - 1)), dma((KVL, 3, NX - 1)),
        ],
        compiler_params=pltpu.CompilerParams(
            collective_id=0, has_side_effects=True, vmem_limit_bytes=48 * 1024 * 1024
        ),
        name="attention_backward",
    )(lengths, queries, keys, values, out_grad)


def solution(mesh):
    spec = P(("seq", "head"), None)
    return jax.shard_map(
        functools.partial(on_device, mesh.shape["seq"]),
        mesh=mesh,
        in_specs=(spec, spec, spec, spec, P()),
        out_specs=(spec, spec, spec),
        check_vma=False,
    )
```

```python
import functools
import math

import jax
import jax.numpy as jnp
from jax import lax
from jax.experimental import pallas as pl
from jax.experimental.pallas import tpu as pltpu
from jax.sharding import PartitionSpec as P

MESH = pl.DeviceIdType.MESH
HD = 128
U = 96
NX = 4
SH = NX * U
REACH = 4
WIN = (REACH + 1) * SH
KVL = 2
GR = 4
QT = 256
TILES = GR * SH // QT
ROWS = 17 * U
COLS = GR * SH
NEG = -1e30
SCALE = 1.0 / math.sqrt(HD)
EXP2_SCALE = SCALE * math.log2(math.e)
NT = (((1,), (1,)), ((), ()))
TN = (((0,), (0,)), ((), ()))
F32 = jnp.float32
BF16 = jnp.bfloat16


def kernel(
    n_seq,
    lengths, q_in, k_in, v_in, o_in,
    dq_out, dk_out, dv_out,
    kvw, qb, ob, qst, ost, s_buf, d_buf, p_all, s_all, acc, stage, landed, dq_stage, final,
    local_sem, kv_send, kv_recv, qo_send, qo_recv, ctx_send, ctx_recv, ret_send, ret_recv,
    out_send, out_recv,
):
    s = lax.axis_index("seq")
    x = lax.axis_index("head")
    core = lax.rem(s, 2)
    sibling = s + 1 - 2 * core
    ahead = lax.rem(s + 2, n_seq)
    behind = lax.rem(s + n_seq - 2, n_seq)
    ahead_far = lax.rem(s + 4, n_seq)
    behind_far = lax.rem(s + n_seq - 4, n_seq)
    peers = [lax.rem(x + d, NX) for d in range(NX)]

    barrier = pltpu.get_barrier_semaphore()
    for d in range(1, NX):
        pl.semaphore_signal(barrier, inc=1, device_id=(s, peers[d]), device_id_type=MESH)
    for other in (sibling, ahead, behind, ahead_far, behind_far):
        pl.semaphore_signal(barrier, inc=1, device_id=(other, x), device_id_type=MESH)
    pl.semaphore_wait(barrier, NX + 4)

    def remote(src, dst, send, recv, where):
        return pltpu.make_async_remote_copy(
            src_ref=src, dst_ref=dst, send_sem=send, recv_sem=recv,
            device_id=where, device_id_type=MESH,
        )

    def rows(start, size):
        return pl.ds(pl.multiple_of(start, U), size)

    def lanes(start, size):
        return pl.ds(pl.multiple_of(start, HD), size)

    def kv_copy(h, t, d):
        src = (k_in, v_in)[t].at[:, lanes(peers[d] * KVL * HD + h * HD, HD)]
        dst = kvw.at[h, t, rows(REACH * SH + x * U, U), :]
        if d == 0:
            return pltpu.make_async_copy(src, dst, local_sem.at[h, t])
        i = d - 1
        return remote(src, dst, kv_send.at[h, t, i], kv_recv.at[h, t, i], (s, peers[d]))

    def qo_copy(h, t, d):
        wide = GR * HD
        src = (q_in, o_in)[t].at[:, lanes(peers[d] * KVL * wide + h * wide, wide)]
        dst = (qb, ob)[t].at[h, x]
        if d == 0:
            return pltpu.make_async_copy(src, dst, local_sem.at[h, 2 + t])
        i = d - 1
        return remote(src, dst, qo_send.at[h, t, i], qo_recv.at[h, t, i], (s, peers[d]))

    def shard(rel):
        return rows((REACH + rel) * SH, SH)

    def own_ahead(h):
        return remote(kvw.at[h, :, shard(0), :], kvw.at[h, :, shard(-2), :],
                      ctx_send.at[h, 0], ctx_recv.at[h, 0], (ahead, x))

    def own_far_ahead(h):
        return remote(kvw.at[h, :, shard(0), :], kvw.at[h, :, shard(-4), :],
                      ctx_send.at[h, 1], ctx_recv.at[h, 1], (ahead_far, x))

    def share_near(h):
        return remote(kvw.at[h, :, shard(-2 * core), :], kvw.at[h, :, shard(-1), :],
                      ctx_send.at[h, 2], ctx_recv.at[h, 2], (sibling, x))

    def share_far(h):
        return remote(kvw.at[h, :, shard(-2 - 2 * core), :], kvw.at[h, :, shard(-3), :],
                      ctx_send.at[h, 3], ctx_recv.at[h, 3], (sibling, x))

    for h in range(KVL):
        for copy in (kv_copy, qo_copy):
            for d in (2, 1, 3, 0):
                for t in range(2):
                    copy(h, t, d).start()

    def wait_in(h, copy):
        for t in range(2):
            copy(h, t, 0).wait()
            for d in range(1, NX):
                copy(h, t, d).wait_recv()

    def context_send(h):
        wait_in(h, kv_copy)

        @pl.when(core == 0)
        def _():
            share_near(h).start()

        own_ahead(h).start()
        own_far_ahead(h).start()

    def context_share_near(h):
        own_ahead(h).wait_recv()

        @pl.when(core == 0)
        def _():
            share_far(h).start()

        @pl.when(core == 1)
        def _():
            share_near(h).start()

    def context_share_far(h):
        own_far_ahead(h).wait_recv()

        @pl.when(core == 1)
        def _():
            share_far(h).start()

    def prepare(h):
        wait_in(h, qo_copy)
        for a in range(NX):
            for j in range(GR):
                at = (a * GR + j) * U
                qst[h, at:at + U, :] = qb[h, a, :, j * HD:(j + 1) * HD]
                ost[h, at:at + U, :] = ob[h, a, :, j * HD:(j + 1) * HD]
        share_near(h).wait_recv()
        share_far(h).wait_recv()

    context_send(0)

    first_unit = s * NX - REACH * NX
    starts = [jnp.int32(-(1 << 20))] * NX
    bound = jnp.int32(0)
    starts = [jnp.int32(0) - first_unit] * NX
    for doc in range(lengths.shape[0]):
        bound = bound + lengths[doc]
        starts = [
            jnp.where(bound <= s * NX + a, bound - first_unit, starts[a]) for a in range(NX)
        ]

    for ref in (p_all, s_all):
        ref[0:U, :] = jnp.zeros((U, COLS), BF16)
        ref[U:3 * U, COLS // 2:] = jnp.zeros((2 * U, COLS // 2), BF16)
        ref[18 * U:, :COLS // 2] = jnp.zeros((2 * U, COLS // 2), BF16)

    lane = lax.broadcasted_iota(jnp.int32, (1, QT), 1)
    row = lax.broadcasted_iota(jnp.int32, (U, QT), 0)

    def tile(h, tile_at):
        pair = tile_at // (TILES // 2)
        base = pl.multiple_of((1 + 2 * pair) * U, U)
        cols = tile_at * QT + lane
        unit = cols // (GR * U)
        at = lax.rem(cols, U)
        begin = jnp.zeros((1, QT), jnp.int32)
        for a in range(NX):
            begin = jnp.where(unit == a, starts[a], begin)
        tile_cols = pl.ds(pl.multiple_of(tile_at * QT, QT), QT)
        q_tile = qst[h, tile_cols, :]
        o_tile = ost[h, tile_cols, :]

        def bias(b):
            return jnp.where((begin <= b) & (b <= REACH * NX + unit), 0.0, NEG)

        top = jnp.full((8, QT), -3e38, F32)
        for c in range(ROWS // U):
            b = 1 + 2 * pair + c
            keys = kvw[h, 0, pl.ds(base + c * U, U), :]
            scores = lax.dot_general(keys, q_tile, NT, preferred_element_type=F32)
            if c >= 15:
                ok = (b < REACH * NX + unit) | (row <= at)
                scores = jnp.where(ok, scores, NEG)
            s_buf[c * U:(c + 1) * U, :] = scores
            top = jnp.maximum(top, jnp.max(scores.reshape(U // 8, 8, QT), axis=0) + bias(b))
        top = jnp.max(top, axis=0, keepdims=True)

        total = jnp.zeros((8, QT), F32)
        inner = jnp.zeros((8, QT), F32)
        for c in range(ROWS // U):
            b = 1 + 2 * pair + c
            shift = (bias(b) - top) * EXP2_SCALE
            weights = jnp.exp2(s_buf[c * U:(c + 1) * U, :] * EXP2_SCALE + shift)
            vals = kvw[h, 1, pl.ds(base + c * U, U), :]
            dprobs = lax.dot_general(vals, o_tile, NT, preferred_element_type=F32)
            s_buf[c * U:(c + 1) * U, :] = weights
            d_buf[c * U:(c + 1) * U, :] = dprobs
            total = total + jnp.sum(weights.reshape(U // 8, 8, QT), axis=0)
            inner = inner + jnp.sum((weights * dprobs).reshape(U // 8, 8, QT), axis=0)
        inverse = 1.0 / jnp.sum(total, axis=0, keepdims=True)
        delta = jnp.sum(inner, axis=0, keepdims=True) * inverse

        for c in range(ROWS // U):
            probs = s_buf[c * U:(c + 1) * U, :] * inverse
            dscores = probs * (d_buf[c * U:(c + 1) * U, :] - delta)
            key_rows = pl.ds(base + c * U, U)
            p_all[key_rows, tile_cols] = probs.astype(BF16)
            s_all[key_rows, tile_cols] = dscores.astype(BF16)
        window = pl.ds(base, ROWS)
        dq = lax.dot_general(
            s_all[window, tile_cols], kvw[h, 0, window, :], TN, preferred_element_type=F32
        )
        dq_stage[h, tile_cols, :] = (dq * SCALE).astype(BF16)

    wide = GR * HD

    def dq_copy(h, d):
        src = qb.at[h, peers[d]]
        dst = dq_out.at[:, lanes(x * KVL * wide + h * wide, wide)]
        if d == 0:
            return pltpu.make_async_copy(src, dst, local_sem.at[h, 4])
        return remote(src, dst, out_send.at[h, 0, d - 1], out_recv.at[h, 0, d - 1], (s, peers[d]))

    def dkv_copy(h, t, d):
        src = final.at[h, t, rows(peers[d] * U, U), :]
        dst = (dk_out, dv_out)[t].at[:, lanes(x * KVL * HD + h * HD, HD)]
        if d == 0:
            return pltpu.make_async_copy(src, dst, local_sem.at[h, 5 + t])
        i = d - 1
        return remote(
            src, dst, out_send.at[h, 1 + t, i], out_recv.at[h, 1 + t, i], (s, peers[d])
        )

    def ret_copy(h, n):
        where = ((sibling, x), (sibling, x), (behind_far, x), (behind, x))[n]
        return remote(stage.at[h, n], landed.at[h, n], ret_send.at[h, n], ret_recv.at[h, n], where)

    def put(h, n, rel):
        stage[h, n] = acc[h, :, shard(rel), :].astype(BF16)
        ret_copy(h, n).start()

    def take(h, n, rel):
        ret_copy(h, n).wait_recv()
        acc[h, :, shard(rel), :] += landed[h, n].astype(F32)

    def send_dq(h):
        for a in range(NX):
            for j in range(GR):
                at = (a * GR + j) * U
                qb[h, a, :, j * HD:(j + 1) * HD] = dq_stage[h, at:at + U, :]
        for d in (2, 1, 3, 0):
            dq_copy(h, d).start()

    def key_grads(h, rel):
        at = (REACH + rel) * SH
        acc[h, 1, at:at + SH, :] = jnp.dot(
            p_all[at:at + SH, :], ost[h], preferred_element_type=F32
        )
        acc[h, 0, at:at + SH, :] = jnp.dot(
            s_all[at:at + SH, :], qst[h], preferred_element_type=F32
        )

    def all_key_grads(h):
        key_grads(h, -3)
        put(h, 0, -3)
        key_grads(h, -4)

        @pl.when(core == 1)
        def _():
            take(h, 0, -4)

        put(h, 2, -4)
        key_grads(h, -1)
        put(h, 1, -1)
        key_grads(h, -2)

        @pl.when(core == 0)
        def _():
            take(h, 0, -2)

        @pl.when(core == 1)
        def _():
            take(h, 1, -2)

        put(h, 3, -2)
        key_grads(h, 0)

        @pl.when(core == 0)
        def _():
            take(h, 1, 0)

    def send_dkv(h):
        take(h, 2, 0)
        take(h, 3, 0)
        final[h, 0] = (acc[h, 0, REACH * SH:, :] * SCALE).astype(BF16)
        final[h, 1] = acc[h, 1, REACH * SH:, :].astype(BF16)
        for d in (2, 1, 3, 0):
            for t in range(2):
                dkv_copy(h, t, d).start()

    def tiles(h, hooks):
        def step(i, carry):
            for at, hook in hooks.items():
                pl.when(i == at)(hook)
            tile(h, i)
            return carry

        lax.fori_loop(0, TILES, step, 0)

    context_share_near(0)
    context_share_far(0)
    prepare(0)
    tiles(0, {
        0: lambda: context_send(1),
        2: lambda: context_share_near(1),
        3: lambda: context_share_far(1),
    })
    send_dq(0)
    all_key_grads(0)
    prepare(1)
    tiles(1, {3: lambda: send_dkv(0)})
    send_dq(1)
    all_key_grads(1)
    send_dkv(1)

    for h in range(KVL):
        for d in range(1, NX):
            for t in range(2):
                kv_copy(h, t, d).wait_send()
                qo_copy(h, t, d).wait_send()
                dkv_copy(h, t, d).wait()
            dq_copy(h, d).wait()
        dq_copy(h, 0).wait()
        for t in range(2):
            dkv_copy(h, t, 0).wait()
        for copy in (own_ahead, own_far_ahead, share_near, share_far):
            copy(h).wait_send()
        for n in range(4):
            ret_copy(h, n).wait_send()


def on_device(n_seq, queries, keys, values, out_grad, lengths):
    anywhere = pl.BlockSpec(memory_space=pl.ANY)
    dma = pltpu.SemaphoreType.DMA
    return pl.pallas_call(
        functools.partial(kernel, n_seq),
        out_shape=(
            jax.ShapeDtypeStruct(queries.shape, BF16),
            jax.ShapeDtypeStruct(keys.shape, BF16),
            jax.ShapeDtypeStruct(values.shape, BF16),
        ),
        in_specs=[pl.BlockSpec(memory_space=pltpu.SMEM)] + [anywhere] * 4,
        out_specs=(anywhere,) * 3,
        scratch_shapes=[
            pltpu.VMEM((KVL, 2, WIN, HD), BF16),
            pltpu.VMEM((KVL, NX, U, GR * HD), BF16),
            pltpu.VMEM((KVL, NX, U, GR * HD), BF16),
            pltpu.VMEM((KVL, GR * SH, HD), BF16),
            pltpu.VMEM((KVL, GR * SH, HD), BF16),
            pltpu.VMEM((ROWS, QT), F32),
            pltpu.VMEM((ROWS, QT), F32),
            pltpu.VMEM((WIN, COLS), BF16),
            pltpu.VMEM((WIN, COLS), BF16),
            pltpu.VMEM((KVL, 2, WIN, HD), F32),
            pltpu.VMEM((KVL, 4, 2, SH, HD), BF16),
            pltpu.VMEM((KVL, 4, 2, SH, HD), BF16),
            pltpu.VMEM((KVL, GR * SH, HD), BF16),
            pltpu.VMEM((KVL, 2, SH, HD), BF16),
            dma((KVL, 7)),
            dma((KVL, 2, NX - 1)), dma((KVL, 2, NX - 1)),
            dma((KVL, 2, NX - 1)), dma((KVL, 2, NX - 1)),
            dma((KVL, 4)), dma((KVL, 4)),
            dma((KVL, 4)), dma((KVL, 4)),
            dma((KVL, 3, NX - 1)), dma((KVL, 3, NX - 1)),
        ],
        compiler_params=pltpu.CompilerParams(
            collective_id=0, has_side_effects=True, vmem_limit_bytes=60 * 1024 * 1024
        ),
        name="attention_backward",
    )(lengths, queries, keys, values, out_grad)


def solution(mesh):
    spec = P(("seq", "head"), None)
    return jax.shard_map(
        functools.partial(on_device, mesh.shape["seq"]),
        mesh=mesh,
        in_specs=(spec, spec, spec, spec, P()),
        out_specs=(spec, spec, spec),
        check_vma=False,
    )
```

```python
import functools
import math

import jax
import jax.numpy as jnp
from jax import lax
from jax.experimental import pallas as pl
from jax.experimental.pallas import tpu as pltpu
from jax.sharding import PartitionSpec as P

MESH = pl.DeviceIdType.MESH
HD = 128
U = 96
NX = 4
SH = NX * U
REACH = 4
WIN = (REACH + 1) * SH
KVL = 2
GR = 4
QT = 256
STEP = 4
DEPTH = 256
TILES = GR * SH // QT
ROWS = 17 * U
COLS = GR * SH
NEG = -1e30
SCALE = 1.0 / math.sqrt(HD)
EXP2_SCALE = SCALE * math.log2(math.e)
NT = (((1,), (1,)), ((), ()))
TN = (((0,), (0,)), ((), ()))
F32 = jnp.float32
BF16 = jnp.bfloat16


def kernel(
    n_seq,
    lengths, q_in, k_in, v_in, o_in,
    dq_out, dk_out, dv_out,
    kvw, qb, ob, qst, ost, s_even, d_even, s_odd, d_odd, p_all, s_all, acc, stage, landed, dq_stage, final,
    local_sem, kv_send, kv_recv, qo_send, qo_recv, ctx_send, ctx_recv, ret_send, ret_recv,
    out_send, out_recv,
):
    s = lax.axis_index("seq")
    x = lax.axis_index("head")
    core = lax.rem(s, 2)
    sibling = s + 1 - 2 * core
    ahead = lax.rem(s + 2, n_seq)
    behind = lax.rem(s + n_seq - 2, n_seq)
    ahead_far = lax.rem(s + 4, n_seq)
    behind_far = lax.rem(s + n_seq - 4, n_seq)
    peers = [lax.rem(x + d, NX) for d in range(NX)]

    barrier = pltpu.get_barrier_semaphore()
    for d in range(1, NX):
        pl.semaphore_signal(barrier, inc=1, device_id=(s, peers[d]), device_id_type=MESH)
    for other in (sibling, ahead, behind, ahead_far, behind_far):
        pl.semaphore_signal(barrier, inc=1, device_id=(other, x), device_id_type=MESH)
    pl.semaphore_wait(barrier, NX + 4)

    def remote(src, dst, send, recv, where):
        return pltpu.make_async_remote_copy(
            src_ref=src, dst_ref=dst, send_sem=send, recv_sem=recv,
            device_id=where, device_id_type=MESH,
        )

    def rows(start, size):
        return pl.ds(pl.multiple_of(start, U), size)

    def lanes(start, size):
        return pl.ds(pl.multiple_of(start, HD), size)

    def kv_copy(h, t, d):
        src = (k_in, v_in)[t].at[:, lanes(peers[d] * KVL * HD + h * HD, HD)]
        dst = kvw.at[h, t, rows(REACH * SH + x * U, U), :]
        if d == 0:
            return pltpu.make_async_copy(src, dst, local_sem.at[h, t])
        i = d - 1
        return remote(src, dst, kv_send.at[h, t, i], kv_recv.at[h, t, i], (s, peers[d]))

    def qo_copy(h, t, d):
        wide = GR * HD
        src = (q_in, o_in)[t].at[:, lanes(peers[d] * KVL * wide + h * wide, wide)]
        dst = (qb, ob)[t].at[h, x]
        if d == 0:
            return pltpu.make_async_copy(src, dst, local_sem.at[h, 2 + t])
        i = d - 1
        return remote(src, dst, qo_send.at[h, t, i], qo_recv.at[h, t, i], (s, peers[d]))

    def shard(rel):
        return rows((REACH + rel) * SH, SH)

    def own_ahead(h):
        return remote(kvw.at[h, :, shard(0), :], kvw.at[h, :, shard(-2), :],
                      ctx_send.at[h, 0], ctx_recv.at[h, 0], (ahead, x))

    def own_far_ahead(h):
        return remote(kvw.at[h, :, shard(0), :], kvw.at[h, :, shard(-4), :],
                      ctx_send.at[h, 1], ctx_recv.at[h, 1], (ahead_far, x))

    def share_near(h):
        return remote(kvw.at[h, :, shard(-2 * core), :], kvw.at[h, :, shard(-1), :],
                      ctx_send.at[h, 2], ctx_recv.at[h, 2], (sibling, x))

    def share_far(h):
        return remote(kvw.at[h, :, shard(-2 - 2 * core), :], kvw.at[h, :, shard(-3), :],
                      ctx_send.at[h, 3], ctx_recv.at[h, 3], (sibling, x))

    for h in range(KVL):
        for copy in (kv_copy, qo_copy):
            for d in (2, 1, 3, 0):
                for t in range(2):
                    copy(h, t, d).start()

    def wait_in(h, copy):
        for t in range(2):
            copy(h, t, 0).wait()
            for d in range(1, NX):
                copy(h, t, d).wait_recv()

    def context_send(h):
        wait_in(h, kv_copy)

        @pl.when(core == 0)
        def _():
            share_near(h).start()

        own_ahead(h).start()
        own_far_ahead(h).start()

    def context_share_near(h):
        own_ahead(h).wait_recv()

        @pl.when(core == 0)
        def _():
            share_far(h).start()

        @pl.when(core == 1)
        def _():
            share_near(h).start()

    def context_share_far(h):
        own_far_ahead(h).wait_recv()

        @pl.when(core == 1)
        def _():
            share_far(h).start()

    def prepare(h):
        wait_in(h, qo_copy)
        for a in range(NX):
            for j in range(GR):
                at = (a * GR + j) * U
                qst[h, at:at + U, :] = qb[h, a, :, j * HD:(j + 1) * HD]
                ost[h, at:at + U, :] = ob[h, a, :, j * HD:(j + 1) * HD]
        share_near(h).wait_recv()
        share_far(h).wait_recv()

    context_send(0)

    first_unit = s * NX - REACH * NX
    starts = [jnp.int32(-(1 << 20))] * NX
    bound = jnp.int32(0)
    starts = [jnp.int32(0) - first_unit] * NX
    for doc in range(lengths.shape[0]):
        bound = bound + lengths[doc]
        starts = [
            jnp.where(bound <= s * NX + a, bound - first_unit, starts[a]) for a in range(NX)
        ]

    s_all[...] = jnp.zeros_like(s_all)
    lane = lax.broadcasted_iota(jnp.int32, (1, QT), 1)
    row = lax.broadcasted_iota(jnp.int32, (U, QT), 0)
    units = ROWS // U

    def fold(array, how):
        return how(array.reshape(U // 8, 8, QT), axis=0)

    def geometry(tile_at):
        pair = tile_at // (TILES // 2)
        cols = tile_at * QT + lane
        unit = cols // (GR * U)
        begin = jnp.zeros((1, QT), jnp.int32)
        for a in range(NX):
            begin = jnp.where(unit == a, starts[a], begin)
        first = 1 + 2 * pair

        def bias(c):
            b = first + c
            return jnp.where((begin <= b) & (b <= REACH * NX + unit), 0.0, NEG)

        def ok(c):
            return (first + c < REACH * NX + unit) | (row <= lax.rem(cols, U))

        return (
            pl.multiple_of(first * U, U),
            pl.ds(pl.multiple_of(tile_at * QT, QT), QT),
            bias,
            ok,
        )

    def scores_stage(h, tile_at, sb, db):
        base, cols, bias, ok = geometry(tile_at)
        out = {"top": jnp.full((8, QT), -3e38, F32)}
        pieces = []

        def scores_piece(at, count):
            q_tile = qst[h, cols, :]
            keys = kvw[h, 0, pl.ds(base + at * U, count * U), :]
            scores = lax.dot_general(keys, q_tile, NT, preferred_element_type=F32)
            for k in range(count):
                c = at + k
                part = scores[k * U:(k + 1) * U, :]
                if c >= units - 2:
                    part = jnp.where(ok(c), part, NEG)
                sb[c * U:(c + 1) * U, :] = part
                out["top"] = jnp.maximum(out["top"], fold(part, jnp.max) + bias(c))

        def dprobs_piece(at, count):
            vals = kvw[h, 1, pl.ds(base + at * U, count * U), :]
            db[at * U:(at + count) * U, :] = lax.dot_general(
                vals, ost[h, cols, :], NT, preferred_element_type=F32
            )

        for at in range(0, units, STEP):
            count = min(STEP, units - at)
            pieces.append(functools.partial(scores_piece, at, count))
        for at in range(0, units, STEP):
            count = min(STEP, units - at)
            pieces.append(functools.partial(dprobs_piece, at, count))
        return pieces, out

    def exp_stage(tile_at, sb, db, top):
        _, _, bias, _ = geometry(tile_at)
        top = jnp.max(top, axis=0, keepdims=True)
        out = {"total": jnp.zeros((8, QT), F32), "inner": jnp.zeros((8, QT), F32)}

        def piece(c):
            shift = (bias(c) - top) * EXP2_SCALE
            weights = jnp.exp2(sb[c * U:(c + 1) * U, :] * EXP2_SCALE + shift)
            sb[c * U:(c + 1) * U, :] = weights
            out["total"] = out["total"] + fold(weights, jnp.sum)
            out["inner"] = out["inner"] + fold(weights * db[c * U:(c + 1) * U, :], jnp.sum)

        return [functools.partial(piece, c) for c in range(units)], out

    def grad_stage(tile_at, sb, db, sums):
        base, cols, _, _ = geometry(tile_at)
        inverse = 1.0 / jnp.sum(sums["total"], axis=0, keepdims=True)
        delta = jnp.sum(sums["inner"], axis=0, keepdims=True) * inverse

        def piece(c):
            probs = sb[c * U:(c + 1) * U, :] * inverse
            dscores = probs * (db[c * U:(c + 1) * U, :] - delta)
            key_rows = pl.ds(base + c * U, U)
            p_all[key_rows, cols] = probs.astype(BF16)
            s_all[key_rows, cols] = dscores.astype(BF16)

        return [functools.partial(piece, c) for c in range(units)]

    def query_stage(h, tile_at):
        base, cols, _, _ = geometry(tile_at)
        out = {"dq": None}

        def piece(at, size):
            part = lax.dot_general(
                s_all[pl.ds(base + at, size), cols],
                kvw[h, 0, pl.ds(base + at, size), :],
                TN,
                preferred_element_type=F32,
            )
            out["dq"] = part if out["dq"] is None else out["dq"] + part
            if at + size == ROWS:
                dq_stage[h, cols, :] = (out["dq"] * SCALE).astype(BF16)

        return [
            functools.partial(piece, at, min(DEPTH, ROWS - at)) for at in range(0, ROWS, DEPTH)
        ]

    def together(*stages):
        order = [
            ((n + 0.5) / len(stage), which, piece)
            for which, stage in enumerate(stages)
            for n, piece in enumerate(stage)
        ]
        for _, _, piece in sorted(order, key=lambda entry: entry[:2]):
            piece()

    wide = GR * HD

    def dq_copy(h, d):
        src = qb.at[h, peers[d]]
        dst = dq_out.at[:, lanes(x * KVL * wide + h * wide, wide)]
        if d == 0:
            return pltpu.make_async_copy(src, dst, local_sem.at[h, 4])
        return remote(src, dst, out_send.at[h, 0, d - 1], out_recv.at[h, 0, d - 1], (s, peers[d]))

    def dkv_copy(h, t, d):
        src = final.at[h, t, rows(peers[d] * U, U), :]
        dst = (dk_out, dv_out)[t].at[:, lanes(x * KVL * HD + h * HD, HD)]
        if d == 0:
            return pltpu.make_async_copy(src, dst, local_sem.at[h, 5 + t])
        i = d - 1
        return remote(
            src, dst, out_send.at[h, 1 + t, i], out_recv.at[h, 1 + t, i], (s, peers[d])
        )

    def ret_copy(h, n):
        where = ((sibling, x), (sibling, x), (behind_far, x), (behind, x))[n]
        return remote(stage.at[h, n], landed.at[h, n], ret_send.at[h, n], ret_recv.at[h, n], where)

    def put(h, n, rel):
        stage[h, n] = acc[h, :, shard(rel), :].astype(BF16)
        ret_copy(h, n).start()

    def take(h, n, rel):
        ret_copy(h, n).wait_recv()
        acc[h, :, shard(rel), :] += landed[h, n].astype(F32)

    def send_dq(h):
        for a in range(NX):
            for j in range(GR):
                at = (a * GR + j) * U
                qb[h, a, :, j * HD:(j + 1) * HD] = dq_stage[h, at:at + U, :]
        for d in (2, 1, 3, 0):
            dq_copy(h, d).start()

    def key_grads(h, rel):
        half = COLS // 2
        at = (REACH + rel) * SH
        parts = [(at, at + SH, 0, COLS)]
        if rel == -REACH:
            acc[h, :, 0:U, :] = jnp.zeros((2, U, HD), F32)
            parts = [(U, 3 * U, 0, half), (3 * U, SH, 0, COLS)]
        if rel == 0:
            parts = [(at, at + 2 * U, 0, COLS), (at + 2 * U, at + SH, half, COLS)]
        for top, end, left, right in parts:
            acc[h, 1, top:end, :] = jnp.dot(
                p_all[top:end, left:right], ost[h, left:right, :], preferred_element_type=F32
            )
            acc[h, 0, top:end, :] = jnp.dot(
                s_all[top:end, left:right], qst[h, left:right, :], preferred_element_type=F32
            )

    def all_key_grads(h):
        key_grads(h, -3)
        put(h, 0, -3)
        key_grads(h, -4)

        @pl.when(core == 1)
        def _():
            take(h, 0, -4)

        put(h, 2, -4)
        key_grads(h, -1)
        put(h, 1, -1)
        key_grads(h, -2)

        @pl.when(core == 0)
        def _():
            take(h, 0, -2)

        @pl.when(core == 1)
        def _():
            take(h, 1, -2)

        put(h, 3, -2)
        key_grads(h, 0)

        @pl.when(core == 0)
        def _():
            take(h, 1, 0)

    def send_dkv(h):
        take(h, 2, 0)
        take(h, 3, 0)
        final[h, 0] = (acc[h, 0, REACH * SH:, :] * SCALE).astype(BF16)
        final[h, 1] = acc[h, 1, REACH * SH:, :].astype(BF16)
        for d in (2, 1, 3, 0):
            for t in range(2):
                dkv_copy(h, t, d).start()

    def tiles(h, hooks):
        even, odd = (s_even, d_even), (s_odd, d_odd)
        pieces, first = scores_stage(h, 0, *even)
        together(pieces)

        def step(i, top):
            for at, hook in hooks.items():
                pl.when(i == at)(hook)
            for now, here, there in ((2 * i, even, odd), (2 * i + 1, odd, even)):
                before = jnp.maximum(now - 1, 0)
                after = jnp.minimum(now + 1, TILES - 1)
                pieces, sums = exp_stage(now, *here, top)
                together(query_stage(h, before), pieces)
                following, out = scores_stage(h, after, *there)
                together(following, grad_stage(now, *here, sums))
                top = out["top"]
            return top

        lax.fori_loop(0, TILES // 2, step, first["top"])
        together(query_stage(h, TILES - 1))

    context_share_near(0)
    context_share_far(0)
    prepare(0)
    tiles(0, {
        0: lambda: context_send(1),
        1: lambda: context_share_near(1),
        2: lambda: context_share_far(1),
    })
    send_dq(0)
    all_key_grads(0)
    prepare(1)
    tiles(1, {1: lambda: send_dkv(0)})
    send_dq(1)
    all_key_grads(1)
    send_dkv(1)

    for h in range(KVL):
        for d in range(1, NX):
            for t in range(2):
                kv_copy(h, t, d).wait_send()
                qo_copy(h, t, d).wait_send()
                dkv_copy(h, t, d).wait()
            dq_copy(h, d).wait()
        dq_copy(h, 0).wait()
        for t in range(2):
            dkv_copy(h, t, 0).wait()
        for copy in (own_ahead, own_far_ahead, share_near, share_far):
            copy(h).wait_send()
        for n in range(4):
            ret_copy(h, n).wait_send()


def on_device(n_seq, queries, keys, values, out_grad, lengths):
    anywhere = pl.BlockSpec(memory_space=pl.ANY)
    dma = pltpu.SemaphoreType.DMA
    return pl.pallas_call(
        functools.partial(kernel, n_seq),
        out_shape=(
            jax.ShapeDtypeStruct(queries.shape, BF16),
            jax.ShapeDtypeStruct(keys.shape, BF16),
            jax.ShapeDtypeStruct(values.shape, BF16),
        ),
        in_specs=[pl.BlockSpec(memory_space=pltpu.SMEM)] + [anywhere] * 4,
        out_specs=(anywhere,) * 3,
        scratch_shapes=[
            pltpu.VMEM((KVL, 2, WIN, HD), BF16),
            pltpu.VMEM((KVL, NX, U, GR * HD), BF16),
            pltpu.VMEM((KVL, NX, U, GR * HD), BF16),
            pltpu.VMEM((KVL, GR * SH, HD), BF16),
            pltpu.VMEM((KVL, GR * SH, HD), BF16),
            pltpu.VMEM((ROWS, QT), F32),
            pltpu.VMEM((ROWS, QT), F32),
            pltpu.VMEM((ROWS, QT), F32),
            pltpu.VMEM((ROWS, QT), F32),
            pltpu.VMEM((WIN, COLS), BF16),
            pltpu.VMEM((WIN, COLS), BF16),
            pltpu.VMEM((KVL, 2, WIN, HD), F32),
            pltpu.VMEM((KVL, 4, 2, SH, HD), BF16),
            pltpu.VMEM((KVL, 4, 2, SH, HD), BF16),
            pltpu.VMEM((KVL, GR * SH, HD), BF16),
            pltpu.VMEM((KVL, 2, SH, HD), BF16),
            dma((KVL, 7)),
            dma((KVL, 2, NX - 1)), dma((KVL, 2, NX - 1)),
            dma((KVL, 2, NX - 1)), dma((KVL, 2, NX - 1)),
            dma((KVL, 4)), dma((KVL, 4)),
            dma((KVL, 4)), dma((KVL, 4)),
            dma((KVL, 3, NX - 1)), dma((KVL, 3, NX - 1)),
        ],
        compiler_params=pltpu.CompilerParams(
            collective_id=0, has_side_effects=True, vmem_limit_bytes=60 * 1024 * 1024
        ),
        name="attention_backward",
    )(lengths, queries, keys, values, out_grad)


def solution(mesh):
    spec = P(("seq", "head"), None)
    return jax.shard_map(
        functools.partial(on_device, mesh.shape["seq"]),
        mesh=mesh,
        in_specs=(spec, spec, spec, spec, P()),
        out_specs=(spec, spec, spec),
        check_vma=False,
    )
```

```python
import functools
import math

import jax
import jax.numpy as jnp
from jax import lax
from jax.experimental import pallas as pl
from jax.experimental.pallas import tpu as pltpu
from jax.sharding import PartitionSpec as P

MESH = pl.DeviceIdType.MESH
HD = 128
U = 96
NX = 4
SH = NX * U
REACH = 4
WIN = (REACH + 1) * SH
KVL = 2
GR = 4
QT = 256
STEP = 4
PARTS = 2
DEPTH = 256
TILES = GR * SH // QT
ROWS = 17 * U
COLS = GR * SH
NEG = -1e30
SCALE = 1.0 / math.sqrt(HD)
EXP2_SCALE = SCALE * math.log2(math.e)
NT = (((1,), (1,)), ((), ()))
TN = (((0,), (0,)), ((), ()))
F32 = jnp.float32
BF16 = jnp.bfloat16


def kernel(
    n_seq,
    lengths, q_in, k_in, v_in, o_in,
    dq_out, dk_out, dv_out,
    kvw, qb, ob, qst, ost, s_even, d_even, s_odd, d_odd, p_all, s_all, acc, stage, landed, dq_stage, final,
    local_sem, kv_send, kv_recv, qo_send, qo_recv, ctx_send, ctx_recv, ret_send, ret_recv,
    out_send, out_recv,
):
    s = lax.axis_index("seq")
    x = lax.axis_index("head")
    core = lax.rem(s, 2)
    sibling = s + 1 - 2 * core
    ahead = lax.rem(s + 2, n_seq)
    behind = lax.rem(s + n_seq - 2, n_seq)
    ahead_far = lax.rem(s + 4, n_seq)
    behind_far = lax.rem(s + n_seq - 4, n_seq)
    peers = [lax.rem(x + d, NX) for d in range(NX)]

    barrier = pltpu.get_barrier_semaphore()
    for d in range(1, NX):
        pl.semaphore_signal(barrier, inc=1, device_id=(s, peers[d]), device_id_type=MESH)
    for other in (sibling, ahead, behind, ahead_far, behind_far):
        pl.semaphore_signal(barrier, inc=1, device_id=(other, x), device_id_type=MESH)
    pl.semaphore_wait(barrier, NX + 4)

    def remote(src, dst, send, recv, where):
        return pltpu.make_async_remote_copy(
            src_ref=src, dst_ref=dst, send_sem=send, recv_sem=recv,
            device_id=where, device_id_type=MESH,
        )

    def rows(start, size):
        return pl.ds(pl.multiple_of(start, U), size)

    def lanes(start, size):
        return pl.ds(pl.multiple_of(start, HD), size)

    def kv_copy(h, t, d):
        src = (k_in, v_in)[t].at[:, lanes(peers[d] * KVL * HD + h * HD, HD)]
        dst = kvw.at[h, t, rows(REACH * SH + x * U, U), :]
        if d == 0:
            return pltpu.make_async_copy(src, dst, local_sem.at[h, t])
        i = d - 1
        return remote(src, dst, kv_send.at[h, t, i], kv_recv.at[h, t, i], (s, peers[d]))

    def qo_copy(h, t, d):
        wide = GR * HD
        src = (q_in, o_in)[t].at[:, lanes(peers[d] * KVL * wide + h * wide, wide)]
        dst = (qb, ob)[t].at[h, x]
        if d == 0:
            return pltpu.make_async_copy(src, dst, local_sem.at[h, 2 + t])
        i = d - 1
        return remote(src, dst, qo_send.at[h, t, i], qo_recv.at[h, t, i], (s, peers[d]))

    def shard(rel):
        return rows((REACH + rel) * SH, SH)

    def own_ahead(h):
        return remote(kvw.at[h, :, shard(0), :], kvw.at[h, :, shard(-2), :],
                      ctx_send.at[h, 0], ctx_recv.at[h, 0], (ahead, x))

    def own_far_ahead(h):
        return remote(kvw.at[h, :, shard(0), :], kvw.at[h, :, shard(-4), :],
                      ctx_send.at[h, 1], ctx_recv.at[h, 1], (ahead_far, x))

    def share_near(h):
        return remote(kvw.at[h, :, shard(-2 * core), :], kvw.at[h, :, shard(-1), :],
                      ctx_send.at[h, 2], ctx_recv.at[h, 2], (sibling, x))

    def share_far(h):
        return remote(kvw.at[h, :, shard(-2 - 2 * core), :], kvw.at[h, :, shard(-3), :],
                      ctx_send.at[h, 3], ctx_recv.at[h, 3], (sibling, x))

    for copy in (kv_copy, qo_copy):
        for h in range(KVL):
            for d in (2, 1, 3, 0):
                for t in range(2):
                    copy(h, t, d).start()

    def wait_in(h, copy):
        for t in range(2):
            copy(h, t, 0).wait()
            for d in range(1, NX):
                copy(h, t, d).wait_recv()

    def context_send(h):
        wait_in(h, kv_copy)

        @pl.when(core == 0)
        def _():
            share_near(h).start()

        own_ahead(h).start()
        own_far_ahead(h).start()

    def context_share_near(h):
        own_ahead(h).wait_recv()

        @pl.when(core == 0)
        def _():
            share_far(h).start()

        @pl.when(core == 1)
        def _():
            share_near(h).start()

    def context_share_far(h):
        own_far_ahead(h).wait_recv()

        @pl.when(core == 1)
        def _():
            share_far(h).start()

    def prepare(h):
        wait_in(h, qo_copy)
        for a in range(NX):
            for j in range(GR):
                at = (a * GR + j) * U
                qst[h, at:at + U, :] = qb[h, a, :, j * HD:(j + 1) * HD]
                ost[h, at:at + U, :] = ob[h, a, :, j * HD:(j + 1) * HD]
        share_near(h).wait_recv()
        share_far(h).wait_recv()

    context_send(0)
    context_send(1)

    first_unit = s * NX - REACH * NX
    starts = [jnp.int32(-(1 << 20))] * NX
    bound = jnp.int32(0)
    starts = [jnp.int32(0) - first_unit] * NX
    for doc in range(lengths.shape[0]):
        bound = bound + lengths[doc]
        starts = [
            jnp.where(bound <= s * NX + a, bound - first_unit, starts[a]) for a in range(NX)
        ]

    s_all[...] = jnp.zeros_like(s_all)
    lane = lax.broadcasted_iota(jnp.int32, (1, QT), 1)
    row = lax.broadcasted_iota(jnp.int32, (U, QT), 0)
    units = ROWS // U

    def fold(array, how):
        return how(array.reshape(U // 8, 8, QT), axis=0)

    def geometry(tile_at):
        pair = tile_at // (TILES // 2)
        cols = tile_at * QT + lane
        unit = cols // (GR * U)
        begin = jnp.zeros((1, QT), jnp.int32)
        for a in range(NX):
            begin = jnp.where(unit == a, starts[a], begin)
        first = 1 + 2 * pair

        def bias(c):
            b = first + c
            return jnp.where((begin <= b) & (b <= REACH * NX + unit), 0.0, NEG)

        def ok(c):
            return (first + c < REACH * NX + unit) | (row <= lax.rem(cols, U))

        return (
            pl.multiple_of(first * U, U),
            pl.ds(pl.multiple_of(tile_at * QT, QT), QT),
            bias,
            ok,
        )

    def scores_stage(h, tile_at, sb, db):
        base, cols, bias, ok = geometry(tile_at)
        out = {"top": jnp.full((8, QT), -3e38, F32)}
        pieces = []

        def scores_piece(at, count):
            q_tile = qst[h, cols, :]
            keys = kvw[h, 0, pl.ds(base + at * U, count * U), :]
            scores = lax.dot_general(keys, q_tile, NT, preferred_element_type=F32)
            for k in range(count):
                c = at + k
                part = scores[k * U:(k + 1) * U, :]
                if c >= units - 2:
                    part = jnp.where(ok(c), part, NEG)
                sb[c * U:(c + 1) * U, :] = part
                out["top"] = jnp.maximum(out["top"], fold(part, jnp.max) + bias(c))

        def dprobs_piece(at, count):
            vals = kvw[h, 1, pl.ds(base + at * U, count * U), :]
            db[at * U:(at + count) * U, :] = lax.dot_general(
                vals, ost[h, cols, :], NT, preferred_element_type=F32
            )

        for at in range(0, units, STEP):
            count = min(STEP, units - at)
            pieces.append(functools.partial(scores_piece, at, count))
        for at in range(0, units, STEP):
            count = min(STEP, units - at)
            pieces.append(functools.partial(dprobs_piece, at, count))
        return pieces, out

    def exp_stage(tile_at, sb, db, top):
        _, _, bias, _ = geometry(tile_at)
        top = jnp.max(top, axis=0, keepdims=True)
        out = {"total": jnp.zeros((8, QT), F32), "inner": jnp.zeros((8, QT), F32)}

        def piece(c):
            shift = (bias(c) - top) * EXP2_SCALE
            weights = jnp.exp2(sb[c * U:(c + 1) * U, :] * EXP2_SCALE + shift)
            sb[c * U:(c + 1) * U, :] = weights
            out["total"] = out["total"] + fold(weights, jnp.sum)
            out["inner"] = out["inner"] + fold(weights * db[c * U:(c + 1) * U, :], jnp.sum)

        return [functools.partial(piece, c) for c in range(units)], out

    def grad_stage(tile_at, sb, db, sums):
        base, cols, _, _ = geometry(tile_at)
        inverse = 1.0 / jnp.sum(sums["total"], axis=0, keepdims=True)
        delta = jnp.sum(sums["inner"], axis=0, keepdims=True) * inverse

        def piece(c):
            probs = sb[c * U:(c + 1) * U, :] * inverse
            dscores = probs * (db[c * U:(c + 1) * U, :] - delta)
            key_rows = pl.ds(base + c * U, U)
            p_all[key_rows, cols] = probs.astype(BF16)
            s_all[key_rows, cols] = dscores.astype(BF16)

        return [functools.partial(piece, c) for c in range(units)]

    def query_stage(h, tile_at):
        base, cols, _, _ = geometry(tile_at)
        out = {"dq": None}

        def piece(at, size):
            part = lax.dot_general(
                s_all[pl.ds(base + at, size), cols],
                kvw[h, 0, pl.ds(base + at, size), :],
                TN,
                preferred_element_type=F32,
            )
            out["dq"] = part if out["dq"] is None else out["dq"] + part
            if at + size == ROWS:
                dq_stage[h, cols, :] = (out["dq"] * SCALE).astype(BF16)

        return [
            functools.partial(piece, at, min(DEPTH, ROWS - at)) for at in range(0, ROWS, DEPTH)
        ]

    def together(*stages):
        order = [
            ((n + 0.5) / len(stage), which, piece)
            for which, stage in enumerate(stages)
            for n, piece in enumerate(stage)
        ]
        for _, _, piece in sorted(order, key=lambda entry: entry[:2]):
            piece()

    wide = GR * HD

    def dq_copy(h, d):
        src = qb.at[h, peers[d]]
        dst = dq_out.at[:, lanes(x * KVL * wide + h * wide, wide)]
        if d == 0:
            return pltpu.make_async_copy(src, dst, local_sem.at[h, 4])
        return remote(src, dst, out_send.at[h, 0, d - 1], out_recv.at[h, 0, d - 1], (s, peers[d]))

    def dkv_copy(h, t, d):
        src = final.at[h, t, rows(peers[d] * U, U), :]
        dst = (dk_out, dv_out)[t].at[:, lanes(x * KVL * HD + h * HD, HD)]
        if d == 0:
            return pltpu.make_async_copy(src, dst, local_sem.at[h, 5 + t])
        i = d - 1
        return remote(
            src, dst, out_send.at[h, 1 + t, i], out_recv.at[h, 1 + t, i], (s, peers[d])
        )

    def ret_copy(h, n):
        where = ((sibling, x), (sibling, x), (behind_far, x), (behind, x))[n]
        return remote(stage.at[h, n], landed.at[h, n], ret_send.at[h, n], ret_recv.at[h, n], where)

    def put(h, n, rel):
        stage[h, n] = acc[h, :, shard(rel), :].astype(BF16)
        ret_copy(h, n).start()

    def take(h, n, rel):
        ret_copy(h, n).wait_recv()
        acc[h, :, shard(rel), :] += landed[h, n].astype(F32)

    def send_dq(h):
        for a in range(NX):
            for j in range(GR):
                at = (a * GR + j) * U
                qb[h, a, :, j * HD:(j + 1) * HD] = dq_stage[h, at:at + U, :]
        for d in (2, 1, 3, 0):
            dq_copy(h, d).start()

    def key_grads(h, rel):
        half = COLS // 2
        at = (REACH + rel) * SH
        parts = [(at, at + SH, 0, COLS)]
        if rel == -REACH:
            acc[h, :, 0:U, :] = jnp.zeros((2, U, HD), F32)
            parts = [(U, 3 * U, 0, half), (3 * U, SH, 0, COLS)]
        if rel == 0:
            parts = [(at, at + 2 * U, 0, COLS), (at + 2 * U, at + SH, half, COLS)]
        for top, end, left, right in parts:
            acc[h, 1, top:end, :] = jnp.dot(
                p_all[top:end, left:right], ost[h, left:right, :], preferred_element_type=F32
            )
            acc[h, 0, top:end, :] = jnp.dot(
                s_all[top:end, left:right], qst[h, left:right, :], preferred_element_type=F32
            )

    def all_key_grads(h):
        key_grads(h, -3)
        put(h, 0, -3)
        key_grads(h, -1)
        put(h, 1, -1)
        key_grads(h, -4)

        @pl.when(core == 1)
        def _():
            take(h, 0, -4)

        put(h, 2, -4)
        key_grads(h, -2)

        @pl.when(core == 0)
        def _():
            take(h, 0, -2)

        @pl.when(core == 1)
        def _():
            take(h, 1, -2)

        put(h, 3, -2)
        key_grads(h, 0)

        @pl.when(core == 0)
        def _():
            take(h, 1, 0)

    def send_dkv(h):
        take(h, 2, 0)
        take(h, 3, 0)
        final[h, 0] = (acc[h, 0, REACH * SH:, :] * SCALE).astype(BF16)
        final[h, 1] = acc[h, 1, REACH * SH:, :].astype(BF16)
        for d in (2, 1, 3, 0):
            for t in range(2):
                dkv_copy(h, t, d).start()

    def tiles(h, hooks):
        even, odd = (s_even, d_even), (s_odd, d_odd)
        pieces, first = scores_stage(h, 0, *even)
        together(pieces)

        def step(i, top):
            for at, hook in hooks.items():
                pl.when(i == at)(hook)
            for now, here, there in ((2 * i, even, odd), (2 * i + 1, odd, even)):
                before = jnp.maximum(now - 1, 0)
                after = jnp.minimum(now + 1, TILES - 1)
                pieces, sums = exp_stage(now, *here, top)
                together(query_stage(h, before), pieces)
                following, out = scores_stage(h, after, *there)
                together(following, grad_stage(now, *here, sums))
                top = out["top"]
            return top

        lax.fori_loop(0, TILES // 2, step, first["top"])
        together(query_stage(h, TILES - 1))

    context_share_near(0)
    context_share_far(0)
    prepare(0)
    tiles(0, {
        1: lambda: context_share_near(1),
        2: lambda: context_share_far(1),
    })
    send_dq(0)
    all_key_grads(0)
    prepare(1)
    tiles(1, {})
    send_dq(1)
    send_dkv(0)
    all_key_grads(1)
    send_dkv(1)

    for h in range(KVL):
        for d in range(1, NX):
            for t in range(2):
                kv_copy(h, t, d).wait_send()
                qo_copy(h, t, d).wait_send()
                dkv_copy(h, t, d).wait()
            dq_copy(h, d).wait()
        dq_copy(h, 0).wait()
        for t in range(2):
            dkv_copy(h, t, 0).wait()
        for copy in (own_ahead, own_far_ahead, share_near, share_far):
            copy(h).wait_send()
        for n in range(4):
            ret_copy(h, n).wait_send()


def place(dq, dk, dv, dq_out, dk_out, dv_out, dq_held, dk_held, dv_held, sems):
    held = (dq_held, dk_held, dv_held)
    moves = []
    for n in range(PARTS):
        rows = pl.ds(n * (U // PARTS), U // PARTS)
        for i, (src, dst) in enumerate(((dq, dq_out), (dk, dk_out), (dv, dv_out))):
            here = held[i].at[rows, :]
            moves.append((
                pltpu.make_async_copy(src.at[rows, :], here, sems.at[0, n, i]),
                pltpu.make_async_copy(here, dst.at[rows, :], sems.at[1, n, i]),
            ))
    for load, _ in moves:
        load.start()
    for load, store in moves:
        load.wait()
        store.start()
    for _, store in moves:
        store.wait()


def on_device(n_seq, queries, keys, values, out_grad, lengths):
    anywhere = pl.BlockSpec(memory_space=pl.ANY)
    dma = pltpu.SemaphoreType.DMA
    results = pl.pallas_call(
        functools.partial(kernel, n_seq),
        out_shape=(
            jax.ShapeDtypeStruct(queries.shape, BF16),
            jax.ShapeDtypeStruct(keys.shape, BF16),
            jax.ShapeDtypeStruct(values.shape, BF16),
        ),
        in_specs=[pl.BlockSpec(memory_space=pltpu.SMEM)] + [anywhere] * 4,
        out_specs=(anywhere,) * 3,
        scratch_shapes=[
            pltpu.VMEM((KVL, 2, WIN, HD), BF16),
            pltpu.VMEM((KVL, NX, U, GR * HD), BF16),
            pltpu.VMEM((KVL, NX, U, GR * HD), BF16),
            pltpu.VMEM((KVL, GR * SH, HD), BF16),
            pltpu.VMEM((KVL, GR * SH, HD), BF16),
            pltpu.VMEM((ROWS, QT), F32),
            pltpu.VMEM((ROWS, QT), F32),
            pltpu.VMEM((ROWS, QT), F32),
            pltpu.VMEM((ROWS, QT), F32),
            pltpu.VMEM((WIN, COLS), BF16),
            pltpu.VMEM((WIN, COLS), BF16),
            pltpu.VMEM((KVL, 2, WIN, HD), F32),
            pltpu.VMEM((KVL, 4, 2, SH, HD), BF16),
            pltpu.VMEM((KVL, 4, 2, SH, HD), BF16),
            pltpu.VMEM((KVL, GR * SH, HD), BF16),
            pltpu.VMEM((KVL, 2, SH, HD), BF16),
            dma((KVL, 7)),
            dma((KVL, 2, NX - 1)), dma((KVL, 2, NX - 1)),
            dma((KVL, 2, NX - 1)), dma((KVL, 2, NX - 1)),
            dma((KVL, 4)), dma((KVL, 4)),
            dma((KVL, 4)), dma((KVL, 4)),
            dma((KVL, 3, NX - 1)), dma((KVL, 3, NX - 1)),
        ],
        compiler_params=pltpu.CompilerParams(
            collective_id=0, has_side_effects=True, vmem_limit_bytes=60 * 1024 * 1024
        ),
        name="attention_backward",
    )(lengths, queries, keys, values, out_grad)
    return pl.pallas_call(
        place,
        out_shape=tuple(jax.ShapeDtypeStruct(r.shape, r.dtype) for r in results),
        in_specs=[anywhere] * 3,
        out_specs=(anywhere,) * 3,
        scratch_shapes=[pltpu.VMEM(r.shape, r.dtype) for r in results]
        + [dma((2, PARTS, 3))],
        name="place_results",
    )(*results)


def solution(mesh):
    spec = P(("seq", "head"), None)
    return jax.shard_map(
        functools.partial(on_device, mesh.shape["seq"]),
        mesh=mesh,
        in_specs=(spec, spec, spec, spec, P()),
        out_specs=(spec, spec, spec),
        check_vma=False,
    )
```

```python
import functools
import math

import jax
import jax.numpy as jnp
from jax import lax
from jax.experimental import pallas as pl
from jax.experimental.pallas import tpu as pltpu
from jax.sharding import PartitionSpec as P

MESH = pl.DeviceIdType.MESH
HD = 128
U = 96
NX = 4
SH = NX * U
REACH = 4
WIN = (REACH + 1) * SH
KVL = 2
GR = 4
QT = 256
STEP = 9
PARTS = 2
DEPTH = 256
TILES = GR * SH // QT
ROWS = 17 * U
COLS = GR * SH
NEG = -1e30
SCALE = 1.0 / math.sqrt(HD)
NT = (((1,), (1,)), ((), ()))
TN = (((0,), (0,)), ((), ()))
F32 = jnp.float32
BF16 = jnp.bfloat16


def kernel(
    n_seq,
    lengths, q_in, k_in, v_in, o_in,
    dq_out, dk_out, dv_out,
    kvw, qb, ob, qst, ost, s_even, d_even, s_odd, d_odd, p_all, s_all, acc, stage, landed, parts, dq_stage, final,
    local_sem, kv_send, kv_recv, qo_send, qo_recv, ctx_send, ctx_recv, ret_send, ret_recv,
    out_send, out_recv, part_send, part_recv,
):
    s = lax.axis_index("seq")
    x = lax.axis_index("head")
    core = lax.rem(s, 2)
    sibling = s + 1 - 2 * core
    ahead = lax.rem(s + 2, n_seq)
    behind = lax.rem(s + n_seq - 2, n_seq)
    ahead_far = lax.rem(s + 4, n_seq)
    behind_far = lax.rem(s + n_seq - 4, n_seq)
    peers = [x, x + 1 - 2 * lax.rem(x, 2), lax.rem(x + 2, NX), NX - 1 - x]
    own_pair = x // 2
    other_pair = 1 - own_pair

    barrier = pltpu.get_barrier_semaphore()
    for d in range(1, NX):
        pl.semaphore_signal(barrier, inc=1, device_id=(s, peers[d]), device_id_type=MESH)
    pl.semaphore_signal(barrier, inc=1, device_id=(sibling, x), device_id_type=MESH)
    for other in (ahead, behind, ahead_far, behind_far):
        for d in range(NX):
            pl.semaphore_signal(barrier, inc=1, device_id=(other, peers[d]), device_id_type=MESH)
    pl.semaphore_wait(barrier, 5 * NX)

    def remote(src, dst, send, recv, where):
        return pltpu.make_async_remote_copy(
            src_ref=src, dst_ref=dst, send_sem=send, recv_sem=recv,
            device_id=where, device_id_type=MESH,
        )

    def rows(start, size):
        return pl.ds(pl.multiple_of(start, U), size)

    def lanes(start, size):
        return pl.ds(pl.multiple_of(start, HD), size)

    def kv_copy(h, t, d):
        src = (k_in, v_in)[t].at[:, lanes(peers[d] * KVL * HD + h * HD, HD)]
        dst = kvw.at[h, t, rows(REACH * SH + x * U, U), :]
        if d == 0:
            return pltpu.make_async_copy(src, dst, local_sem.at[h, t])
        i = d - 1
        return remote(src, dst, kv_send.at[h, t, i], kv_recv.at[h, t, i], (s, peers[d]))

    def qo_copy(h, t, d):
        wide = GR * HD
        src = (q_in, o_in)[t].at[:, lanes(peers[d] * KVL * wide + h * wide, wide)]
        dst = (qb, ob)[t].at[h, x]
        if d == 0:
            return pltpu.make_async_copy(src, dst, local_sem.at[h, 2 + t])
        i = d - 1
        return remote(src, dst, qo_send.at[h, t, i], qo_recv.at[h, t, i], (s, peers[d]))

    def shard(rel):
        return rows((REACH + rel) * SH, SH)

    def own_ahead(h):
        return remote(kvw.at[h, :, shard(0), :], kvw.at[h, :, shard(-2), :],
                      ctx_send.at[h, 0], ctx_recv.at[h, 0], (ahead, x))

    def own_far_ahead(h):
        return remote(kvw.at[h, :, shard(0), :], kvw.at[h, :, shard(-4), :],
                      ctx_send.at[h, 1], ctx_recv.at[h, 1], (ahead_far, x))

    def share_near(h):
        return remote(kvw.at[h, :, shard(-2 * core), :], kvw.at[h, :, shard(-1), :],
                      ctx_send.at[h, 2], ctx_recv.at[h, 2], (sibling, x))

    def share_far(h):
        return remote(kvw.at[h, :, shard(-2 - 2 * core), :], kvw.at[h, :, shard(-3), :],
                      ctx_send.at[h, 3], ctx_recv.at[h, 3], (sibling, x))

    for copy in (kv_copy, qo_copy):
        for h in range(KVL):
            for d in (2, 3, 1, 0):
                for t in range(2):
                    copy(h, t, d).start()

    def wait_in(h, copy):
        for t in range(2):
            copy(h, t, 0).wait()
            for d in range(1, NX):
                copy(h, t, d).wait_recv()

    def context_send(h):
        wait_in(h, kv_copy)

        @pl.when(core == 0)
        def _():
            share_near(h).start()

        own_ahead(h).start()
        own_far_ahead(h).start()

    def context_share_near(h):
        own_ahead(h).wait_recv()

        @pl.when(core == 0)
        def _():
            share_far(h).start()

        @pl.when(core == 1)
        def _():
            share_near(h).start()

    def context_share_far(h):
        own_far_ahead(h).wait_recv()

        @pl.when(core == 1)
        def _():
            share_far(h).start()

    def take_queries(h, pair, dists):
        for t in range(2):
            for d in dists:
                if d == 0:
                    qo_copy(h, t, d).wait()
                else:
                    qo_copy(h, t, d).wait_recv()
        for k in range(2):
            a = 2 * pair + k
            for j in range(GR):
                at = rows((a * GR + j) * U, U)
                qst[h, at, :] = qb[h, a, :, j * HD:(j + 1) * HD]
                ost[h, at, :] = ob[h, a, :, j * HD:(j + 1) * HD]

    def prepare(h):
        take_queries(h, other_pair, (2, 3))
        take_queries(h, own_pair, (1, 0))
        share_near(h).wait_recv()
        share_far(h).wait_recv()

    context_send(0)
    context_send(1)

    first_unit = s * NX - REACH * NX
    starts = [jnp.int32(-(1 << 20))] * NX
    bound = jnp.int32(0)
    starts = [jnp.int32(0) - first_unit] * NX
    for doc in range(lengths.shape[0]):
        bound = bound + lengths[doc]
        starts = [
            jnp.where(bound <= s * NX + a, bound - first_unit, starts[a]) for a in range(NX)
        ]

    s_all[...] = jnp.zeros_like(s_all)
    lane = lax.broadcasted_iota(jnp.int32, (1, QT), 1)
    row = lax.broadcasted_iota(jnp.int32, (U, QT), 0)
    units = ROWS // U

    def fold(array, how):
        return how(array.reshape(U // 8, 8, QT), axis=0)

    def geometry(tile_at):
        pair = tile_at // (TILES // 2)
        cols = tile_at * QT + lane
        unit = cols // (GR * U)
        begin = jnp.zeros((1, QT), jnp.int32)
        for a in range(NX):
            begin = jnp.where(unit == a, starts[a], begin)
        first = 1 + 2 * pair

        def bias(c):
            b = first + c
            live = begin <= b
            if c >= units - 2:
                live = live & (b <= REACH * NX + unit)
            return jnp.where(live, 0.0, NEG)

        def ok(c):
            return (first + c < REACH * NX + unit) | (row <= lax.rem(cols, U))

        return (
            pl.multiple_of(first * U, U),
            pl.ds(pl.multiple_of(tile_at * QT, QT), QT),
            bias,
            ok,
        )

    def scores_stage(h, tile_at, sb, db):
        base, cols, bias, ok = geometry(tile_at)
        out = {"top": jnp.full((8, QT), -3e38, F32)}
        pieces = []

        def scores_piece(at, count):
            q_tile = qst[h, cols, :]
            keys = kvw[h, 0, pl.ds(base + at * U, count * U), :]
            scores = lax.dot_general(keys, q_tile, NT, preferred_element_type=F32)
            for k in range(count):
                c = at + k
                part = scores[k * U:(k + 1) * U, :]
                if c >= units - 2:
                    part = jnp.where(ok(c), part, NEG)
                sb[c * U:(c + 1) * U, :] = part
                out["top"] = jnp.maximum(out["top"], fold(part, jnp.max) + bias(c))
            if at + count == units:
                out["top"] = jnp.max(out["top"], axis=0, keepdims=True) * SCALE

        def dprobs_piece(at, count):
            vals = kvw[h, 1, pl.ds(base + at * U, count * U), :]
            db[at * U:(at + count) * U, :] = lax.dot_general(
                vals, ost[h, cols, :], NT, preferred_element_type=F32
            )

        for at in range(0, units, STEP):
            count = min(STEP, units - at)
            pieces.append(functools.partial(scores_piece, at, count))
        for at in range(0, units, STEP):
            count = min(STEP, units - at)
            pieces.append(functools.partial(dprobs_piece, at, count))
        return pieces, out

    def exp_stage(tile_at, sb, db, top):
        _, _, bias, _ = geometry(tile_at)
        out = {"total": jnp.zeros((8, QT), F32), "inner": jnp.zeros((8, QT), F32)}

        def piece(c):
            weights = jnp.exp(sb[c * U:(c + 1) * U, :] * SCALE + (bias(c) - top))
            sb[c * U:(c + 1) * U, :] = weights
            out["total"] = out["total"] + fold(weights, jnp.sum)
            out["inner"] = out["inner"] + fold(weights * db[c * U:(c + 1) * U, :], jnp.sum)

        return [functools.partial(piece, c) for c in range(units)], out

    def grad_stage(tile_at, sb, db, sums):
        base, cols, _, _ = geometry(tile_at)
        inverse = 1.0 / jnp.sum(sums["total"], axis=0, keepdims=True)
        delta = jnp.sum(sums["inner"], axis=0, keepdims=True) * inverse

        def piece(c):
            probs = sb[c * U:(c + 1) * U, :] * inverse
            dscores = probs * (db[c * U:(c + 1) * U, :] - delta)
            key_rows = pl.ds(base + c * U, U)
            p_all[key_rows, cols] = probs.astype(BF16)
            s_all[key_rows, cols] = dscores.astype(BF16)

        return [functools.partial(piece, c) for c in range(units)]

    def query_stage(h, tile_at):
        base, cols, _, _ = geometry(tile_at)
        out = {"dq": None}

        def piece(at, size):
            part = lax.dot_general(
                s_all[pl.ds(base + at, size), cols],
                kvw[h, 0, pl.ds(base + at, size), :],
                TN,
                preferred_element_type=F32,
            )
            out["dq"] = part if out["dq"] is None else out["dq"] + part
            if at + size == ROWS:
                dq_stage[h, cols, :] = (out["dq"] * SCALE).astype(BF16)

        return [
            functools.partial(piece, at, min(DEPTH, ROWS - at)) for at in range(0, ROWS, DEPTH)
        ]

    def together(*stages):
        order = [
            ((n + 0.5) / len(stage), which, piece)
            for which, stage in enumerate(stages)
            for n, piece in enumerate(stage)
        ]
        for _, _, piece in sorted(order, key=lambda entry: entry[:2]):
            piece()

    wide = GR * HD

    def dq_copy(h, d):
        src = qb.at[h, peers[d]]
        dst = dq_out.at[:, lanes(x * KVL * wide + h * wide, wide)]
        if d == 0:
            return pltpu.make_async_copy(src, dst, local_sem.at[h, 4])
        return remote(src, dst, out_send.at[h, 0, d - 1], out_recv.at[h, 0, d - 1], (s, peers[d]))

    def part_copy(h, kind, d):
        src = stage.at[h, 2 + kind, :, rows(peers[d] * U, U), :]
        dst = parts.at[h, kind, d]
        if kind == 2 and d == 0:
            return pltpu.make_async_copy(src, dst, local_sem.at[h, 5])
        where = (behind_far, behind, s)[kind]
        return remote(
            src, dst, part_send.at[h, kind, d], part_recv.at[h, kind, d], (where, peers[d])
        )

    def result_copy(t):
        return pltpu.make_async_copy(final.at[t], (dk_out, dv_out)[t], local_sem.at[t, 6])

    def ret_copy(h, n):
        return remote(
            stage.at[h, n], landed.at[h, n], ret_send.at[h, n], ret_recv.at[h, n], (sibling, x)
        )

    def put_parts(h, kind, rel):
        stage[h, 2 + kind] = acc[h, :, shard(rel), :].astype(BF16)
        for d in (2, 3, 1, 0):
            part_copy(h, kind, d).start()

    def put(h, n, rel):
        stage[h, n] = acc[h, :, shard(rel), :].astype(BF16)
        ret_copy(h, n).start()

    def take(h, n, rel):
        ret_copy(h, n).wait_recv()
        acc[h, :, shard(rel), :] += landed[h, n].astype(F32)

    def send_dq(h, pair, dists):
        for k in range(2):
            a = 2 * pair + k
            for j in range(GR):
                at = rows((a * GR + j) * U, U)
                qb[h, a, :, j * HD:(j + 1) * HD] = dq_stage[h, at, :]
        for d in dists:
            dq_copy(h, d).start()

    def key_grads(h, rel):
        half = COLS // 2
        at = (REACH + rel) * SH
        parts = [(at, at + SH, 0, COLS)]
        if rel == -REACH:
            acc[h, :, 0:U, :] = jnp.zeros((2, U, HD), F32)
            parts = [(U, 3 * U, 0, half), (3 * U, SH, 0, COLS)]
        if rel == 0:
            parts = [(at, at + 2 * U, 0, COLS), (at + 2 * U, at + SH, half, COLS)]
        for top, end, left, right in parts:
            acc[h, 1, top:end, :] = jnp.dot(
                p_all[top:end, left:right], ost[h, left:right, :], preferred_element_type=F32
            )
            acc[h, 0, top:end, :] = jnp.dot(
                s_all[top:end, left:right], qst[h, left:right, :], preferred_element_type=F32
            )

    def take_far(h):
        @pl.when(core == 1)
        def _():
            take(h, 0, -4)

        put_parts(h, 0, -4)

    def take_near(h):
        @pl.when(core == 0)
        def _():
            take(h, 0, -2)

        @pl.when(core == 1)
        def _():
            take(h, 1, -2)

        put_parts(h, 1, -2)

    def take_own(h):
        @pl.when(core == 0)
        def _():
            take(h, 1, 0)

        put_parts(h, 2, 0)

    def take_all(h):
        take_far(h)
        take_near(h)
        take_own(h)

    def all_key_grads(h, last):
        key_grads(h, -3)
        put(h, 0, -3)
        key_grads(h, -1)
        put(h, 1, -1)
        key_grads(h, -4)
        if last:
            take_far(h)
        key_grads(h, -2)
        if last:
            take_near(h)
        key_grads(h, 0)
        if last:
            take_own(h)

    def finish(h):
        for kind in (2, 0, 1):
            for d in range(NX):
                if kind == 2 and d == 0:
                    part_copy(h, kind, d).wait()
                else:
                    part_copy(h, kind, d).wait_recv()
        for d in range(NX):
            at = lanes(peers[d] * KVL * HD + h * HD, HD)
            whole = (
                parts[h, 0, d].astype(F32) + parts[h, 1, d].astype(F32) + parts[h, 2, d].astype(F32)
            )
            final[0, :, at] = (whole[0] * SCALE).astype(BF16)
            final[1, :, at] = whole[1].astype(BF16)

    def tiles(h, hooks):
        even, odd = (s_even, d_even), (s_odd, d_odd)
        pieces, first = scores_stage(h, 0, *even)
        together(pieces)

        def step(i, top):
            for at, hook in hooks:
                pl.when(i == at)(hook)
            for now, here, there in ((2 * i, even, odd), (2 * i + 1, odd, even)):
                before = jnp.maximum(now - 1, 0)
                after = jnp.minimum(now + 1, TILES - 1)
                pieces, sums = exp_stage(now, *here, top)
                together(query_stage(h, before), pieces)
                following, out = scores_stage(h, after, *there)
                together(following, grad_stage(now, *here, sums))
                top = out["top"]
            return top

        lax.fori_loop(0, TILES // 2, step, first["top"])
        together(query_stage(h, TILES - 1))

    context_share_near(0)
    context_share_far(0)
    prepare(0)
    tiles(0, [(1, lambda: context_share_near(1)), (2, lambda: context_share_far(1))])
    send_dq(0, other_pair, (2, 3))
    send_dq(0, own_pair, (1, 0))
    all_key_grads(0, False)
    prepare(1)
    tiles(1, [(0, lambda: take_all(0))])
    send_dq(1, other_pair, (2, 3))
    send_dq(1, own_pair, (1, 0))
    all_key_grads(1, True)
    finish(0)
    finish(1)
    for t in range(2):
        result_copy(t).start()

    for h in range(KVL):
        for d in range(1, NX):
            for t in range(2):
                kv_copy(h, t, d).wait_send()
                qo_copy(h, t, d).wait_send()
            dq_copy(h, d).wait()
        dq_copy(h, 0).wait()
        for copy in (own_ahead, own_far_ahead, share_near, share_far):
            copy(h).wait_send()
        for n in range(2):
            ret_copy(h, n).wait_send()
        for kind in range(3):
            for d in range(NX):
                if kind < 2 or d > 0:
                    part_copy(h, kind, d).wait_send()
    for t in range(2):
        result_copy(t).wait()


def place(dq, dk, dv, dq_out, dk_out, dv_out, dq_held, dk_held, dv_held, sems):
    held = (dq_held, dk_held, dv_held)
    moves = []
    for n in range(PARTS):
        rows = pl.ds(n * (U // PARTS), U // PARTS)
        for i, (src, dst) in enumerate(((dq, dq_out), (dk, dk_out), (dv, dv_out))):
            here = held[i].at[rows, :]
            moves.append((
                pltpu.make_async_copy(src.at[rows, :], here, sems.at[0, n, i]),
                pltpu.make_async_copy(here, dst.at[rows, :], sems.at[1, n, i]),
            ))
    for load, _ in moves:
        load.start()
    for load, store in moves:
        load.wait()
        store.start()
    for _, store in moves:
        store.wait()


def on_device(n_seq, queries, keys, values, out_grad, lengths):
    anywhere = pl.BlockSpec(memory_space=pl.ANY)
    dma = pltpu.SemaphoreType.DMA
    results = pl.pallas_call(
        functools.partial(kernel, n_seq),
        out_shape=(
            jax.ShapeDtypeStruct(queries.shape, BF16),
            jax.ShapeDtypeStruct(keys.shape, BF16),
            jax.ShapeDtypeStruct(values.shape, BF16),
        ),
        in_specs=[pl.BlockSpec(memory_space=pltpu.SMEM)] + [anywhere] * 4,
        out_specs=(anywhere,) * 3,
        scratch_shapes=[
            pltpu.VMEM((KVL, 2, WIN, HD), BF16),
            pltpu.VMEM((KVL, NX, U, GR * HD), BF16),
            pltpu.VMEM((KVL, NX, U, GR * HD), BF16),
            pltpu.VMEM((KVL, GR * SH, HD), BF16),
            pltpu.VMEM((KVL, GR * SH, HD), BF16),
            pltpu.VMEM((ROWS, QT), F32),
            pltpu.VMEM((ROWS, QT), F32),
            pltpu.VMEM((ROWS, QT), F32),
            pltpu.VMEM((ROWS, QT), F32),
            pltpu.VMEM((WIN, COLS), BF16),
            pltpu.VMEM((WIN, COLS), BF16),
            pltpu.VMEM((KVL, 2, WIN, HD), F32),
            pltpu.VMEM((KVL, 5, 2, SH, HD), BF16),
            pltpu.VMEM((KVL, 2, 2, SH, HD), BF16),
            pltpu.VMEM((KVL, 3, NX, 2, U, HD), BF16),
            pltpu.VMEM((KVL, GR * SH, HD), BF16),
            pltpu.VMEM((2, U, NX * KVL * HD), BF16),
            dma((KVL, 7)),
            dma((KVL, 2, NX - 1)), dma((KVL, 2, NX - 1)),
            dma((KVL, 2, NX - 1)), dma((KVL, 2, NX - 1)),
            dma((KVL, 4)), dma((KVL, 4)),
            dma((KVL, 2)), dma((KVL, 2)),
            dma((KVL, 1, NX - 1)), dma((KVL, 1, NX - 1)),
            dma((KVL, 3, NX)), dma((KVL, 3, NX)),
        ],
        compiler_params=pltpu.CompilerParams(
            collective_id=0, has_side_effects=True, vmem_limit_bytes=60 * 1024 * 1024
        ),
        name="attention_backward",
    )(lengths, queries, keys, values, out_grad)
    return pl.pallas_call(
        place,
        out_shape=tuple(jax.ShapeDtypeStruct(r.shape, r.dtype) for r in results),
        in_specs=[anywhere] * 3,
        out_specs=(anywhere,) * 3,
        scratch_shapes=[pltpu.VMEM(r.shape, r.dtype) for r in results]
        + [dma((2, PARTS, 3))],
        name="place_results",
    )(*results)


def solution(mesh):
    spec = P(("seq", "head"), None)
    return jax.shard_map(
        functools.partial(on_device, mesh.shape["seq"]),
        mesh=mesh,
        in_specs=(spec, spec, spec, spec, P()),
        out_specs=(spec, spec, spec),
        check_vma=False,
    )
```
